32 devices in a mesh: grp: 8 (over z, x), sp: 4 (over y, core).
Axes of the slice: x: 2, y: 2, z: 4, core: 2. Of those that a mesh axis runs over, the one named last changes fastest.
Arguments:
- vis_feats: bfloat16 [2048, 1152], P('grp'), may hold values from -6 to 6
- proj_w: bfloat16 [1152, 4096], P(None, 'sp'), may hold values from -0.1875 to 0.1875
- text_embed: bfloat16 [8192, 4096], P('grp', 'sp'), may hold values from -6 to 6
- dest_group: int32 [2048], replicated, may hold values from 0 to 7, as said below
- layout: int32 [8, 1024], P('grp'), may hold values from 0 to 1023, each once within a row
- norm_gain: float32 [4096], P('sp'), may hold values from 0.1 to 1.9
- key_w: bfloat16 [4096, 512], P('sp'), may hold values from -0.09375 to 0.09375
- value_w: bfloat16 [4096, 512], P('sp'), may hold values from -0.09375 to 0.09375
Outputs:
- key_out: bfloat16 [8192, 512], P(('grp', 'sp'))
- value_out: bfloat16 [8192, 512], P(('grp', 'sp'))
The draws below stay inside these ranges and needn't reach their ends.
Inputs may be any that keep to these rules, and one draw needn't show every extreme that they name: `dest_group`: each block of 256 rows (one encoder shard's tokens) is 4 runs of 64 consecutive rows; a run names one group, and the runs of one block name distinct groups.
All inputs are finite; a program needn't handle non-finite values.
Results may differ from the reference program's by a relative error of at most 0.024.
Values may be sent and summed in bfloat16 or wider, within the bound.
A program may use at most 64 MiB of HBM per device.

```python
import jax
import jax.numpy as jnp
from jax import lax

D = 4096
VW = 1152
KVW = 512
SEQ = 1024
NV = 2048
RUNS = 4
CAP = 64
N_GRP = 8
N_SP = 4


def draw_dest_group(key, part):
    shard_keys = jax.random.split(key, N_GRP)

    def one_shard(shard_key):
        return jax.random.permutation(shard_key, N_GRP)[:RUNS]
    run_groups = jax.vmap(one_shard)(shard_keys)
    return jnp.repeat(run_groups, CAP, axis=1).reshape(-1).astype(jnp.int32)


def block_levels(stream_key, dims, cuts, smallest, top_value):
    level, own = 1.0, jax.random.fold_in(stream_key, 6)
    for position, shards_of in cuts:
        steps = jnp.exp(jax.random.uniform(jax.random.fold_in(own, position), (shards_of,), jnp.float32, smallest / len(cuts), top_value / len(cuts)))
        level = level * jnp.repeat(steps, dims[position] // shards_of).reshape([-1 if axis == position else 1 for axis in range(len(dims))])
    return level


def centred(key, extent, width, bound, shards=(), kind=jnp.bfloat16):
    values = width * jax.random.normal(key, extent, jnp.float32)
    if shards:
        values = values * block_levels(key, extent, shards, -0.22, 0.18)
    return jnp.clip(values, -bound, bound).astype(kind)


def setup_inputs(seed: int = 0) -> dict:
    streams_of = jax.random.split(jax.random.key(seed), 9)
    return {
        "vis_feats": centred(streams_of[0], (NV, VW), 1.0, 6.0, ((0, 8),)),
        "proj_w": centred(streams_of[1], (VW, D), VW ** -0.5, 0.1875, ((1, 4),)),
        "text_embed": centred(streams_of[2], (N_GRP * SEQ, D), 1.0, 6.0, ((0, 8), (1, 4))),
        "dest_group": draw_dest_group(jax.random.fold_in(streams_of[8], 71), 0),
        "layout": jax.vmap(lambda own: jax.random.permutation(own, SEQ))(jax.random.split(streams_of[4], N_GRP)).reshape((N_GRP, SEQ)).astype(jnp.int32),
        "norm_gain": jnp.clip(1.0 + 0.18 * jax.random.normal(streams_of[5], (D,), jnp.float32), 0.1, 1.9),
        "key_w": centred(streams_of[6], (D, KVW), D ** -0.5, 0.09375, ((0, 4),)),
        "value_w": centred(streams_of[7], (D, KVW), D ** -0.5, 0.09375, ((0, 4),)),
    }


def reference(vis_feats, proj_w, text_embed, dest_group, layout, norm_gain, key_w, value_w):
    vis_proj = jnp.dot(vis_feats, proj_w, preferred_element_type=jnp.float32).astype(jnp.bfloat16)
    width_local = D // N_SP
    kv_weight = jnp.concatenate([key_w, value_w], axis=1).reshape(N_SP, width_local, 2 * KVW).astype(jnp.float32)

    def per_group(grp_idx):
        to_group = dest_group == grp_idx
        slot_rank = jnp.cumsum(to_group.astype(jnp.int32)) - 1
        order_row = lax.dynamic_index_in_dim(layout, grp_idx, 0, keepdims=False)
        positions = jnp.where(to_group, order_row[jnp.clip(slot_rank, 0, SEQ - 1)], SEQ).astype(jnp.int32)
        sequence = lax.dynamic_slice_in_dim(text_embed, (grp_idx * SEQ).astype(jnp.int32), SEQ, 0)
        sequence = sequence.at[positions].set(vis_proj, mode='drop')
        sequence_f = sequence.astype(jnp.float32)
        mean_sq = lax.optimization_barrier(jnp.mean(sequence_f * sequence_f, axis=1))
        scaled = (sequence_f * norm_gain).astype(jnp.bfloat16)
        blocks = scaled.reshape(SEQ, N_SP, width_local).astype(jnp.float32)
        partials = jnp.einsum('sjd,jdc->jsc', blocks, kv_weight).astype(jnp.bfloat16)
        partials = lax.optimization_barrier(partials)
        key_value = lax.optimization_barrier(jnp.sum(partials.astype(jnp.float32), axis=0))
        inv_rms = lax.rsqrt(mean_sq + 1e-05)[:, None]
        key_part = (key_value[:, :KVW] * inv_rms).astype(jnp.bfloat16)
        value_part = (key_value[:, KVW:] * inv_rms).astype(jnp.bfloat16)
        return (key_part, value_part)
    key_all, value_all = lax.map(per_group, jnp.arange(N_GRP, dtype=jnp.int32))
    return (key_all.reshape(N_GRP * SEQ, KVW), value_all.reshape(N_GRP * SEQ, KVW))
```

```python
import functools

import jax
import jax.numpy as jnp
from jax import lax
from jax.experimental import pallas as pl
from jax.experimental.pallas import tpu as pltpu
from jax.sharding import PartitionSpec as P

EPS = 1e-05
MESH = pl.DeviceIdType.MESH
F32 = jnp.float32
BF16 = jnp.bfloat16


def as_row(column):
    return jnp.broadcast_to(column, (column.shape[0], 128)).T[:8]


def as_column(row):
    return jnp.broadcast_to(row[:1], (128, row.shape[1])).T


def kernel(
    dims,
    dest, lay, gain, vis_hbm, proj_hbm, text_hbm, key_hbm, value_hbm,
    key_out, value_out,
    vis, proj, text, weight,
    tok, tok_own, tok_send, tok_recv, tok_sq, tok_sq_recv, tok_done,
    out, ranked, onehot,
    part, core_recv, y_send, y_recv, row_sq, row_sq_recv,
    load_sem, tsq_send_sem, tsq_recv_sem, tok_send_sem, tok_recv_sem,
    out_sem, arr_sem, sq_send_sem, sq_recv_sem,
    core_send_sem, core_recv_sem, y_send_sem, y_recv_sem,
    *arrived,
):
    groups, sps, runs, cap, pad, chunks, width = dims
    ys = sps // 2
    g = lax.axis_index("grp")
    s = lax.axis_index("sp")
    y, core = s // 2, lax.rem(s, 2)
    other = 1 - core
    twin = y * 2 + other
    rows = part.shape[4]
    ranks = groups * pad
    features = text.shape[1]
    total_features = features * sps

    def load(source, target, index):
        copy = pltpu.make_async_copy(source, target, load_sem.at[index])
        copy.start()
        return copy

    load_vis = load(vis_hbm, vis, 0)
    load_proj = load(proj_hbm, proj, 1)
    load_key = load(key_hbm, weight.at[0], 2)
    load_value = load(value_hbm, weight.at[1], 3)
    load_text = load(text_hbm, text, 4)

    barrier = pltpu.get_barrier_semaphore()

    def greet_group(d, carry):
        pl.semaphore_signal(barrier, inc=1, device_id={"grp": lax.rem(g + d, groups)}, device_id_type=MESH)
        return carry

    def greet_sp(d, carry):
        pl.semaphore_signal(barrier, inc=1, device_id={"sp": lax.rem(s + d, sps)}, device_id_type=MESH)
        return carry

    lax.fori_loop(1, groups, greet_group, 0)
    lax.fori_loop(1, sps, greet_sp, 0)

    senders, earlier, count = [], [], jnp.int32(0)
    for source in range(groups):
        found = jnp.int32(0)
        for r in range(runs):
            found = found + (dest[(source * runs + r) * cap] == g).astype(jnp.int32)
        senders.append(found)
        earlier.append(count)
        count = count + found
    n_senders = count
    order = []
    for b in range(groups):
        place_of = jnp.int32(0)
        for source in range(b, groups):
            hit = senders[source] * (earlier[source] == b).astype(jnp.int32)
            place_of = place_of + hit * lax.rem(g - source + groups, groups)
        order.append(jnp.minimum(place_of, groups - 1))
    heads = [dest[(g * runs + r) * cap] for r in range(runs)]

    load_vis.wait()
    load_proj.wait()
    tile = min(256, features)

    def project(n, total):
        columns = pl.ds(pl.multiple_of(n * tile, tile), tile)
        block = jnp.dot(vis[...], proj[:, columns], preferred_element_type=F32).astype(BF16).astype(F32)
        tok[:, columns] = (block * gain[:, columns]).astype(BF16)
        return total + jnp.sum(block * block, axis=1, keepdims=True)

    squares = lax.fori_loop(0, features // tile, project, jnp.zeros((vis.shape[0], 1), F32))
    tok_sq[...] = as_row(squares)
    pl.semaphore_wait(barrier, groups - 1 + sps - 1)

    def token_square_copy(j):
        return pltpu.make_async_remote_copy(
            src_ref=tok_sq, dst_ref=tok_sq_recv.at[j],
            send_sem=tsq_send_sem.at[j], recv_sem=tsq_recv_sem.at[j],
            device_id={"sp": lax.rem(s + j, sps)}, device_id_type=MESH,
        )

    lax.fori_loop(1, sps, lambda j, c: (token_square_copy(j).start(), c)[1], 0)

    def twin_copy(k):
        return pltpu.make_async_remote_copy(
            src_ref=tok_send.at[k], dst_ref=tok_recv.at[k],
            send_sem=tok_send_sem.at[k], recv_sem=tok_recv_sem.at[k],
            device_id={"sp": twin}, device_id_type=MESH,
        )

    load_key.wait()
    load_value.wait()
    for k in range(chunks):
        columns = pl.ds(k * width, width)
        tok_send[k] = jnp.dot(tok[...], weight[other, :, columns], preferred_element_type=F32).astype(BF16)
        twin_copy(k).start()
    for k in range(chunks):
        columns = pl.ds(k * width, width)
        tok_own[k] = jnp.dot(tok[...], weight[core, :, columns], preferred_element_type=F32)

    load_text.wait()
    rank_index = lax.broadcasted_iota(jnp.int32, (1, ranks), 1)
    position_of = jnp.where(rank_index < n_senders * pad, lay[:, :ranks], -1)

    def place(q, carry):
        at = pl.ds(pl.multiple_of(q * rows, rows), rows)
        position = lax.broadcasted_iota(jnp.int32, (rows, ranks), 0) + q * rows
        hit = (position == position_of).astype(F32)
        onehot[at, :] = hit.astype(BF16)
        keep = 1.0 - jnp.max(hit, axis=1, keepdims=True)
        values = text[at, :].astype(F32)
        row_sq[q] = as_row(jnp.sum(values * values, axis=1, keepdims=True))
        text[at, :] = (values * gain[...] * keep).astype(BF16)
        return carry

    lax.fori_loop(0, sps, place, 0)

    def square_copy(j):
        partner = lax.rem(s + j, sps)
        return pltpu.make_async_remote_copy(
            src_ref=row_sq.at[partner], dst_ref=row_sq_recv.at[j],
            send_sem=sq_send_sem.at[j], recv_sem=sq_recv_sem.at[j],
            device_id={"sp": partner}, device_id_type=MESH,
        )

    lax.fori_loop(1, sps, lambda j, c: (square_copy(j).start(), c)[1], 0)

    def gather_token_squares(j, total):
        token_square_copy(j).wait()
        return total + tok_sq_recv[j]

    total = lax.fori_loop(1, sps, gather_token_squares, tok_sq[...])
    token_scale = as_column(lax.rsqrt(total / total_features + EPS))

    def group_copy(k, d):
        return pltpu.make_async_remote_copy(
            src_ref=out.at[k, d], dst_ref=arrived[k].at[d],
            send_sem=out_sem.at[k, d], recv_sem=arr_sem.at[k, d],
            device_id={"grp": lax.rem(g + d, groups)}, device_id_type=MESH,
        )

    def run_for(h):
        run = jnp.int32(0)
        for r in range(1, runs):
            run = run + r * (heads[r] == h).astype(jnp.int32)
        return jnp.minimum(run, runs - 1)

    for k in range(chunks):
        twin_copy(k).wait()
        done = ((tok_own[k] + tok_recv[k].astype(F32)) * token_scale).astype(BF16)
        tok_done[k] = done.reshape(runs, pad, width)
        arrived[k][0] = tok_done[k, run_for(g)]

        def send(d, carry):
            out[k, d] = tok_done[k, run_for(lax.rem(g + d, groups))]
            group_copy(k, d).start()
            return carry

        lax.fori_loop(1, groups, send, 0)

    def multiply(q, carry):
        at = pl.ds(pl.multiple_of(q * rows, rows), rows)
        for kind in range(2):
            product = jnp.dot(text[at, :], weight[kind], preferred_element_type=F32).astype(BF16)
            for k in range(chunks):
                part[k, lax.rem(q, 2), q // 2, kind] = product[:, k * width:(k + 1) * width]
        return carry

    lax.fori_loop(0, sps, multiply, 0)

    def core_copy(k):
        return pltpu.make_async_remote_copy(
            src_ref=part.at[k, other], dst_ref=core_recv.at[k],
            send_sem=core_send_sem.at[k], recv_sem=core_recv_sem.at[k],
            device_id={"sp": twin}, device_id_type=MESH,
        )

    def y_copy(k, j):
        return pltpu.make_async_remote_copy(
            src_ref=y_send.at[k, j], dst_ref=y_recv.at[k, j],
            send_sem=y_send_sem.at[k, j], recv_sem=y_recv_sem.at[k, j],
            device_id={"sp": lax.rem(y + j, ys) * 2 + core}, device_id_type=MESH,
        )

    def place_tokens(k, side):
        def one(yy, carry):
            at = pl.ds(pl.multiple_of((yy * 2 + side) * rows, rows), rows)
            tokens = jnp.dot(onehot[at, :], ranked[...], preferred_element_type=F32)
            part[k, side, yy, core] = (part[k, side, yy, core].astype(F32) + tokens).astype(BF16)
            return carry

        lax.fori_loop(0, ys, one, 0)

    for k in range(chunks):
        lax.fori_loop(1, groups, lambda d, c: (group_copy(k, d).wait(), c)[1], 0)

        for b in range(groups):
            ranked[b * pad:(b + 1) * pad, :] = arrived[k][order[b]]
        place_tokens(k, other)
        core_copy(k).start()
        place_tokens(k, core)
        core_copy(k).wait()

        def pass_on(j, carry):
            yy = lax.rem(y + j, ys)
            y_send[k, j] = (part[k, core, yy].astype(F32) + core_recv[k, yy].astype(F32)).astype(BF16)
            y_copy(k, j).start()
            return carry

        lax.fori_loop(1, ys, pass_on, 0)

    def gather_squares(j, total):
        square_copy(j).wait()
        return total + row_sq_recv[j]

    total = lax.fori_loop(1, sps, gather_squares, row_sq[s])
    mine = pl.ds(pl.multiple_of(s * rows, rows), rows)
    visual = jnp.max(onehot[mine, :].astype(F32), axis=1, keepdims=True)
    scale = as_column(lax.rsqrt(total / total_features + EPS))[:, :width]
    scale = jnp.where(visual > 0.5, 1.0, scale)
    for k in range(chunks):
        def add(j, sums):
            y_copy(k, j).wait()
            return sums + y_recv[k, j].astype(F32)

        sums = part[k, core, y].astype(F32) + core_recv[k, y].astype(F32)
        sums = lax.fori_loop(1, ys, add, sums)
        columns = pl.ds(k * width, width)
        key_out[:, columns] = (sums[0] * scale).astype(BF16)
        value_out[:, columns] = (sums[1] * scale).astype(BF16)


def local(groups, sps, vis_feats, proj_w, text_embed, dest_group, layout, norm_gain, key_w, value_w):
    seq_len, features = text_embed.shape
    shard, raw = vis_feats.shape
    runs = groups // 2
    cap = shard // runs
    pad = -(-cap // 16) * 16
    ranked_layout = layout
    if pad != cap:
        vis_feats = jnp.pad(vis_feats.reshape(runs, cap, raw), ((0, 0), (0, pad - cap), (0, 0)))
        vis_feats = vis_feats.reshape(runs * pad, raw)
        ranked_layout = layout[0, : groups * cap].reshape(groups, cap)
        ranked_layout = jnp.pad(ranked_layout, ((0, 0), (0, pad - cap)), constant_values=-1)
        ranked_layout = ranked_layout.reshape(1, groups * pad)
    tokens = runs * pad
    cols = key_w.shape[1]
    width = 128
    chunks = cols // width
    rows = seq_len // sps
    ys = sps // 2
    ranks = groups * pad
    dims = (groups, sps, runs, cap, pad, chunks, width)
    vmem = pl.BlockSpec(memory_space=pltpu.VMEM)
    smem = pl.BlockSpec(memory_space=pltpu.SMEM)
    anywhere = pl.BlockSpec(memory_space=pl.ANY)
    dma = pltpu.SemaphoreType.DMA
    return pl.pallas_call(
        functools.partial(kernel, dims),
        out_shape=[jax.ShapeDtypeStruct((rows, cols), BF16)] * 2,
        in_specs=[smem, vmem, vmem] + [anywhere] * 5,
        out_specs=[vmem, vmem],
        scratch_shapes=[
            pltpu.VMEM((tokens, raw), BF16),
            pltpu.VMEM((raw, features), BF16),
            pltpu.VMEM((seq_len, features), BF16),
            pltpu.VMEM((2, features, cols), BF16),
            pltpu.VMEM((tokens, features), BF16),
            pltpu.VMEM((chunks, tokens, width), F32),
            pltpu.VMEM((chunks, tokens, width), BF16),
            pltpu.VMEM((chunks, tokens, width), BF16),
            pltpu.VMEM((8, tokens), F32),
            pltpu.VMEM((sps, 8, tokens), F32),
            pltpu.VMEM((chunks, runs, pad, width), BF16),
            pltpu.VMEM((chunks, groups, pad, width), BF16),
            pltpu.VMEM((ranks, width), BF16),
            pltpu.VMEM((seq_len, ranks), BF16),
            pltpu.VMEM((chunks, 2, ys, 2, rows, width), BF16),
            pltpu.VMEM((chunks, ys, 2, rows, width), BF16),
            pltpu.VMEM((chunks, ys, 2, rows, width), BF16),
            pltpu.VMEM((chunks, ys, 2, rows, width), BF16),
            pltpu.VMEM((sps, 8, rows), F32),
            pltpu.VMEM((sps, 8, rows), F32),
            dma((5,)),
            dma((sps,)), dma((sps,)),
            dma((chunks,)), dma((chunks,)),
            dma((chunks, groups)), dma((chunks, groups)),
            dma((sps,)), dma((sps,)),
            dma((chunks,)), dma((chunks,)),
            dma((chunks, ys)), dma((chunks, ys)),
        ] + [pltpu.VMEM((groups, pad, width), BF16)] * chunks,
        compiler_params=pltpu.CompilerParams(
            collective_id=0, has_side_effects=True, vmem_limit_bytes=56 * 1024 * 1024
        ),
        cost_estimate=pl.CostEstimate(flops=5 * 10**9, bytes_accessed=8 * 2**20, transcendentals=0),
        name="route_project",
    )(dest_group, ranked_layout, norm_gain.reshape(1, features), vis_feats, proj_w, text_embed, key_w, value_w)


def solution(mesh):
    return jax.shard_map(
        functools.partial(local, mesh.shape["grp"], mesh.shape["sp"]),
        mesh=mesh,
        in_specs=(
            P("grp", None),
            P(None, "sp"),
            P("grp", "sp"),
            P(),
            P("grp", None),
            P("sp"),
            P("sp", None),
            P("sp", None),
        ),
        out_specs=(P(("grp", "sp"), None), P(("grp", "sp"), None)),
        check_vma=False,
    )
```

```python
import functools

import jax
import jax.numpy as jnp
from jax import lax
from jax.experimental import pallas as pl
from jax.experimental.pallas import tpu as pltpu
from jax.sharding import PartitionSpec as P

EPS = 1e-05
MESH = pl.DeviceIdType.MESH
F32 = jnp.float32
BF16 = jnp.bfloat16


def as_row(column):
    return jnp.broadcast_to(column, (column.shape[0], 128)).T[:8]


def as_column(row):
    return jnp.broadcast_to(row[:1], (128, row.shape[1])).T


def kernel(
    dims,
    dest, lay, gain, vis_hbm, proj_hbm, text_hbm, key_hbm, value_hbm,
    result,
    vis, proj, text, weight,
    tok, tok_own, tok_send, tok_recv, tok_y_send, tok_y_recv, tok_sq, tok_sq_recv, tok_done,
    out, ranked, onehot,
    part, core_recv, y_recv, row_sq, row_sq_recv,
    load_sem, tsq_send_sem, tsq_recv_sem, tok_send_sem, tok_recv_sem, tok_y_send_sem, tok_y_recv_sem,
    out_sem, arr_sem, sq_send_sem, sq_recv_sem,
    core_send_sem, core_recv_sem, y_send_sem, y_recv_sem,
    *arrived,
):
    groups, sps, runs, cap, pad, pieces, width = dims
    ys = sps // 2
    share = pieces * width
    g = lax.axis_index("grp")
    s = lax.axis_index("sp")
    y, core = s // 2, lax.rem(s, 2)
    other = 1 - core
    twin = y * 2 + other
    rows = part.shape[5]
    ranks = groups * pad
    features = text.shape[1]
    total_features = features * sps

    def load(source, target, index):
        copy = pltpu.make_async_copy(source, target, load_sem.at[index])
        copy.start()
        return copy

    load_vis = load(vis_hbm, vis, 0)
    load_proj = load(proj_hbm, proj, 1)
    load_key = load(key_hbm, weight.at[0], 2)
    load_value = load(value_hbm, weight.at[1], 3)
    load_text = load(text_hbm, text, 4)

    barrier = pltpu.get_barrier_semaphore()

    def greet_group(d, carry):
        pl.semaphore_signal(barrier, inc=1, device_id={"grp": lax.rem(g + d, groups)}, device_id_type=MESH)
        return carry

    def greet_sp(d, carry):
        pl.semaphore_signal(barrier, inc=1, device_id={"sp": lax.rem(s + d, sps)}, device_id_type=MESH)
        return carry

    lax.fori_loop(1, groups, greet_group, 0)
    lax.fori_loop(1, sps, greet_sp, 0)

    senders, earlier, count = [], [], jnp.int32(0)
    for source in range(groups):
        found = jnp.int32(0)
        for r in range(runs):
            found = found + (dest[(source * runs + r) * cap] == g).astype(jnp.int32)
        senders.append(found)
        earlier.append(count)
        count = count + found
    n_senders = count
    order = []
    for b in range(groups):
        place_of = jnp.int32(0)
        for source in range(b, groups):
            hit = senders[source] * (earlier[source] == b).astype(jnp.int32)
            place_of = place_of + hit * lax.rem(g - source + groups, groups)
        order.append(jnp.minimum(place_of, groups - 1))
    heads = [dest[(g * runs + r) * cap] for r in range(runs)]

    load_vis.wait()
    load_proj.wait()
    tile = min(256, features)

    def project(n, total):
        columns = pl.ds(pl.multiple_of(n * tile, tile), tile)
        block = jnp.dot(vis[...], proj[:, columns], preferred_element_type=F32).astype(BF16).astype(F32)
        tok[:, columns] = (block * gain[:, columns]).astype(BF16)
        return total + jnp.sum(block * block, axis=1, keepdims=True)

    squares = lax.fori_loop(0, features // tile, project, jnp.zeros((vis.shape[0], 1), F32))
    tok_sq[...] = as_row(squares)
    pl.semaphore_wait(barrier, groups - 1 + sps - 1)

    def token_square_copy(j):
        return pltpu.make_async_remote_copy(
            src_ref=tok_sq, dst_ref=tok_sq_recv.at[j],
            send_sem=tsq_send_sem.at[j], recv_sem=tsq_recv_sem.at[j],
            device_id={"sp": lax.rem(s + j, sps)}, device_id_type=MESH,
        )

    lax.fori_loop(1, sps, lambda j, c: (token_square_copy(j).start(), c)[1], 0)

    def twin_copy(yc):
        return pltpu.make_async_remote_copy(
            src_ref=tok_send.at[yc], dst_ref=tok_recv.at[yc],
            send_sem=tok_send_sem.at[yc], recv_sem=tok_recv_sem.at[yc],
            device_id={"sp": twin}, device_id_type=MESH,
        )

    def token_y_copy(j):
        return pltpu.make_async_remote_copy(
            src_ref=tok_y_send.at[j], dst_ref=tok_y_recv.at[j],
            send_sem=tok_y_send_sem.at[j], recv_sem=tok_y_recv_sem.at[j],
            device_id={"sp": lax.rem(y + j, ys) * 2 + core}, device_id_type=MESH,
        )

    load_key.wait()
    load_value.wait()
    product = jnp.dot(tok[...], weight[other], preferred_element_type=F32).astype(BF16)
    for yc in range(ys):
        for p in range(pieces):
            at = yc * share + p * width
            tok_send[yc, p] = product[:, at:at + width]
    lax.fori_loop(1, ys + 1, lambda j, c: (twin_copy(lax.rem(y + j, ys)).start(), c)[1], 0)
    product = jnp.dot(tok[...], weight[core], preferred_element_type=F32)
    for yc in range(ys):
        for p in range(pieces):
            at = yc * share + p * width
            tok_own[yc, p] = product[:, at:at + width]

    def pass_tokens(j, carry):
        yc = lax.rem(y + j, ys)
        twin_copy(yc).wait()
        tok_y_send[j] = (tok_own[yc] + tok_recv[yc].astype(F32)).astype(BF16)
        token_y_copy(j).start()
        return carry

    lax.fori_loop(1, ys, pass_tokens, 0)

    load_text.wait()
    rank_index = lax.broadcasted_iota(jnp.int32, (1, ranks), 1)
    position_of = jnp.where(rank_index < n_senders * pad, lay[:, :ranks], -1)

    def place(q, carry):
        at = pl.ds(pl.multiple_of(q * rows, rows), rows)
        position = lax.broadcasted_iota(jnp.int32, (rows, ranks), 0) + q * rows
        hit = (position == position_of).astype(F32)
        onehot[at, :] = hit.astype(BF16)
        keep = 1.0 - jnp.max(hit, axis=1, keepdims=True)
        values = text[at, :].astype(F32)
        row_sq[q] = as_row(jnp.sum(values * values, axis=1, keepdims=True))
        text[at, :] = (values * gain[...] * keep).astype(BF16)
        return carry

    lax.fori_loop(0, sps, place, 0)

    def square_copy(j):
        partner = lax.rem(s + j, sps)
        return pltpu.make_async_remote_copy(
            src_ref=row_sq.at[partner], dst_ref=row_sq_recv.at[j],
            send_sem=sq_send_sem.at[j], recv_sem=sq_recv_sem.at[j],
            device_id={"sp": partner}, device_id_type=MESH,
        )

    lax.fori_loop(1, sps, lambda j, c: (square_copy(j).start(), c)[1], 0)

    def multiply_share(yc):
        columns = pl.ds(pl.multiple_of(yc * share, share), share)

        def one(q, carry):
            at = pl.ds(pl.multiple_of(q * rows, rows), rows)
            for kind in range(2):
                block = jnp.dot(text[at, :], weight[kind, :, columns], preferred_element_type=F32).astype(BF16)
                for p in range(pieces):
                    part[yc, p, lax.rem(q, 2), q // 2, kind] = block[:, p * width:(p + 1) * width]
            return carry

        lax.fori_loop(0, sps, one, 0)

    def multiply_all(q, carry):
        at = pl.ds(pl.multiple_of(q * rows, rows), rows)
        for kind in range(2):
            block = jnp.dot(text[at, :], weight[kind], preferred_element_type=F32).astype(BF16)
            for yc in range(ys):
                for p in range(pieces):
                    first = yc * share + p * width
                    part[yc, p, lax.rem(q, 2), q // 2, kind] = block[:, first:first + width]
        return carry

    def core_copy(yc, p):
        return pltpu.make_async_remote_copy(
            src_ref=part.at[yc, p, other], dst_ref=core_recv.at[yc, p],
            send_sem=core_send_sem.at[yc, p], recv_sem=core_recv_sem.at[yc, p],
            device_id={"sp": twin}, device_id_type=MESH,
        )

    def y_copy(yc, p, j):
        yy = lax.rem(y + j, ys)
        return pltpu.make_async_remote_copy(
            src_ref=part.at[yc, p, core, yy], dst_ref=y_recv.at[yc, p, j],
            send_sem=y_send_sem.at[yc, p, j], recv_sem=y_recv_sem.at[yc, p, j],
            device_id={"sp": yy * 2 + core}, device_id_type=MESH,
        )

    def pass_on(yc, p):
        core_copy(yc, p).wait()

        def one(j, carry):
            yy = lax.rem(y + j, ys)
            pair = part[yc, p, core, yy].astype(F32) + core_recv[yc, p, yy].astype(F32)
            part[yc, p, core, yy] = pair.astype(BF16)
            y_copy(yc, p, j).start()
            return carry

        lax.fori_loop(1, ys, one, 0)

    by_share = share % 128 == 0
    if not by_share:
        lax.fori_loop(0, sps, multiply_all, 0)

    def other_share(j, carry):
        yc = lax.rem(y + j, ys)
        if by_share:
            multiply_share(yc)
        for p in range(pieces):
            core_copy(yc, p).start()
        return carry

    lax.fori_loop(1, ys, other_share, 0)

    def gather_token_squares(j, total):
        token_square_copy(j).wait()
        return total + tok_sq_recv[j]

    total = lax.fori_loop(1, sps, gather_token_squares, tok_sq[...])
    token_scale = as_column(lax.rsqrt(total / total_features + EPS))[:, :width]

    def group_copy(p, d):
        return pltpu.make_async_remote_copy(
            src_ref=out.at[p, d], dst_ref=arrived[p].at[d],
            send_sem=out_sem.at[p, d], recv_sem=arr_sem.at[p, d],
            device_id={"grp": lax.rem(g + d, groups)}, device_id_type=MESH,
        )

    def run_for(h):
        run = jnp.int32(0)
        for r in range(1, runs):
            run = run + r * (heads[r] == h).astype(jnp.int32)
        return jnp.minimum(run, runs - 1)

    def gather_tokens(j, sums):
        token_y_copy(j).wait()
        return sums + tok_y_recv[j].astype(F32)

    twin_copy(y).wait()
    sums = lax.fori_loop(1, ys, gather_tokens, tok_own[y] + tok_recv[y].astype(F32))
    for p in range(pieces):
        tok_done[p] = (sums[p] * token_scale).astype(BF16).reshape(runs, pad, width)
        arrived[p][0] = tok_done[p, run_for(g)]

        def send(d, carry):
            out[p, d] = tok_done[p, run_for(lax.rem(g + d, groups))]
            group_copy(p, d).start()
            return carry

        lax.fori_loop(1, groups, send, 0)

    def other_pass(j, carry):
        for p in range(pieces):
            pass_on(lax.rem(y + j, ys), p)
        return carry

    lax.fori_loop(1, ys, other_pass, 0)

    if by_share:
        multiply_share(y)

    def place_tokens(p, side):
        def one(yy, carry):
            at = pl.ds(pl.multiple_of((yy * 2 + side) * rows, rows), rows)
            tokens = jnp.dot(onehot[at, :], ranked[...], preferred_element_type=F32)
            part[y, p, side, yy, core] = (part[y, p, side, yy, core].astype(F32) + tokens).astype(BF16)
            return carry

        lax.fori_loop(0, ys, one, 0)

    for p in range(pieces):
        lax.fori_loop(1, groups, lambda d, c: (group_copy(p, d).wait(), c)[1], 0)
        for b in range(groups):
            ranked[b * pad:(b + 1) * pad, :] = arrived[p][order[b]]
        place_tokens(p, other)
        core_copy(y, p).start()
        place_tokens(p, core)
        pass_on(y, p)

    def gather_squares(j, total):
        square_copy(j).wait()
        return total + row_sq_recv[j]

    total = lax.fori_loop(1, sps, gather_squares, row_sq[s])
    mine = pl.ds(pl.multiple_of(s * rows, rows), rows)
    visual = jnp.max(onehot[mine, :].astype(F32), axis=1, keepdims=True)
    scale = as_column(lax.rsqrt(total / total_features + EPS))[:, :width]
    scale = jnp.where(visual > 0.5, 1.0, scale)
    for p in range(pieces):
        for yc in range(ys):
            def add(j, sums):
                y_copy(yc, p, j).wait()
                return sums + y_recv[yc, p, j].astype(F32)

            sums = part[yc, p, core, y].astype(F32) + core_recv[yc, p, y].astype(F32)
            sums = lax.fori_loop(1, ys, add, sums)
            first = yc * share + p * width
            result[0, :, first:first + width] = (sums[0] * scale).astype(BF16)
            result[1, :, first:first + width] = (sums[1] * scale).astype(BF16)


def split(both, key_out, value_out, sem):
    copies = [pltpu.make_async_copy(both.at[i], target, sem.at[i]) for i, target in enumerate((key_out, value_out))]
    for copy in copies:
        copy.start()
    for copy in copies:
        copy.wait()


def local(groups, sps, vis_feats, proj_w, text_embed, dest_group, layout, norm_gain, key_w, value_w):
    seq_len, features = text_embed.shape
    shard, raw = vis_feats.shape
    runs = groups // 2
    cap = shard // runs
    pad = -(-cap // 16) * 16
    ranked_layout = layout
    if pad != cap:
        vis_feats = jnp.pad(vis_feats.reshape(runs, cap, raw), ((0, 0), (0, pad - cap), (0, 0)))
        vis_feats = vis_feats.reshape(runs * pad, raw)
        ranked_layout = layout[0, : groups * cap].reshape(groups, cap)
        ranked_layout = jnp.pad(ranked_layout, ((0, 0), (0, pad - cap)), constant_values=-1)
        ranked_layout = ranked_layout.reshape(1, groups * pad)
    tokens = runs * pad
    cols = key_w.shape[1]
    rows = seq_len // sps
    ys = sps // 2
    width = min(128, cols // ys)
    pieces = cols // (ys * width)
    ranks = groups * pad
    dims = (groups, sps, runs, cap, pad, pieces, width)
    vmem = pl.BlockSpec(memory_space=pltpu.VMEM)
    smem = pl.BlockSpec(memory_space=pltpu.SMEM)
    anywhere = pl.BlockSpec(memory_space=pl.ANY)
    dma = pltpu.SemaphoreType.DMA
    both = pl.pallas_call(
        functools.partial(kernel, dims),
        out_shape=jax.ShapeDtypeStruct((2, rows, cols), BF16),
        in_specs=[smem, vmem, vmem] + [anywhere] * 5,
        out_specs=vmem,
        scratch_shapes=[
            pltpu.VMEM((tokens, raw), BF16),
            pltpu.VMEM((raw, features), BF16),
            pltpu.VMEM((seq_len, features), BF16),
            pltpu.VMEM((2, features, cols), BF16),
            pltpu.VMEM((tokens, features), BF16),
            pltpu.VMEM((ys, pieces, tokens, width), F32),
            pltpu.VMEM((ys, pieces, tokens, width), BF16),
            pltpu.VMEM((ys, pieces, tokens, width), BF16),
            pltpu.VMEM((ys, pieces, tokens, width), BF16),
            pltpu.VMEM((ys, pieces, tokens, width), BF16),
            pltpu.VMEM((8, tokens), F32),
            pltpu.VMEM((sps, 8, tokens), F32),
            pltpu.VMEM((pieces, runs, pad, width), BF16),
            pltpu.VMEM((pieces, groups, pad, width), BF16),
            pltpu.VMEM((ranks, width), BF16),
            pltpu.VMEM((seq_len, ranks), BF16),
            pltpu.VMEM((ys, pieces, 2, ys, 2, rows, width), BF16),
            pltpu.VMEM((ys, pieces, ys, 2, rows, width), BF16),
            pltpu.VMEM((ys, pieces, ys, 2, rows, width), BF16),
            pltpu.VMEM((sps, 8, rows), F32),
            pltpu.VMEM((sps, 8, rows), F32),
            dma((5,)),
            dma((sps,)), dma((sps,)),
            dma((ys,)), dma((ys,)), dma((ys,)), dma((ys,)),
            dma((pieces, groups)), dma((pieces, groups)),
            dma((sps,)), dma((sps,)),
            dma((ys, pieces)), dma((ys, pieces)),
            dma((ys, pieces, ys)), dma((ys, pieces, ys)),
        ] + [pltpu.VMEM((groups, pad, width), BF16)] * pieces,
        compiler_params=pltpu.CompilerParams(
            collective_id=0, has_side_effects=True, vmem_limit_bytes=60 * 1024 * 1024
        ),
        cost_estimate=pl.CostEstimate(flops=5 * 10**9, bytes_accessed=8 * 2**20, transcendentals=0),
        name="route_project",
    )(dest_group, ranked_layout, norm_gain.reshape(1, features), vis_feats, proj_w, text_embed, key_w, value_w)
    return pl.pallas_call(
        split,
        out_shape=[jax.ShapeDtypeStruct((rows, cols), BF16)] * 2,
        in_specs=[anywhere],
        out_specs=[anywhere, anywhere],
        scratch_shapes=[dma((2,))],
        compiler_params=pltpu.CompilerParams(vmem_limit_bytes=60 * 1024 * 1024),
        name="split_result",
    )(both)


def solution(mesh):
    return jax.shard_map(
        functools.partial(local, mesh.shape["grp"], mesh.shape["sp"]),
        mesh=mesh,
        in_specs=(
            P("grp", None),
            P(None, "sp"),
            P("grp", "sp"),
            P(),
            P("grp", None),
            P("sp"),
            P("sp", None),
            P("sp", None),
        ),
        out_specs=(P(("grp", "sp"), None), P(("grp", "sp"), None)),
        check_vma=False,
    )
```

```python
import functools

import jax
import jax.numpy as jnp
from jax import lax
from jax.experimental import pallas as pl
from jax.experimental.pallas import tpu as pltpu
from jax.sharding import PartitionSpec as P

EPS = 1e-05
MESH = pl.DeviceIdType.MESH
F32 = jnp.float32
BF16 = jnp.bfloat16


def as_row(column):
    return jnp.broadcast_to(column, (column.shape[0], 128)).T[:8]


def as_column(row):
    return jnp.broadcast_to(row[:1], (128, row.shape[1])).T


def kernel(
    dims,
    dest, lay, gain, vis_hbm, proj_hbm, text_hbm, key_hbm, value_hbm,
    result,
    vis, proj, text, weight,
    tok, tok_own, tok_send, tok_recv, tok_y_send, tok_y_recv, tok_sq, tok_sq_recv, tok_done,
    out, ranked, onehot,
    part, core_recv, y_recv, row_sq, row_sq_recv,
    load_sem, proj_sem, tsq_send_sem, tsq_recv_sem, tok_send_sem, tok_recv_sem, tok_y_send_sem, tok_y_recv_sem,
    out_sem, arr_sem, sq_send_sem, sq_recv_sem,
    core_send_sem, core_recv_sem, y_send_sem, y_recv_sem,
    *arrived,
):
    groups, sps, runs, cap, pad, pieces, width = dims
    ys = sps // 2
    share = pieces * width
    g = lax.axis_index("grp")
    s = lax.axis_index("sp")
    y, core = s // 2, lax.rem(s, 2)
    other = 1 - core
    twin = y * 2 + other
    rows = part.shape[5]
    ranks = groups * pad
    features = text.shape[1]
    total_features = features * sps

    def load(source, target, index):
        copy = pltpu.make_async_copy(source, target, load_sem.at[index])
        copy.start()
        return copy

    tile = min(256, features)

    def proj_copy(n):
        columns = pl.ds(pl.multiple_of(n * tile, tile), tile)
        return pltpu.make_async_copy(proj_hbm.at[:, columns], proj.at[:, columns], proj_sem.at[n])

    load_vis = load(vis_hbm, vis, 0)
    for n in range(features // tile):
        proj_copy(n).start()
    load_key = load(key_hbm, weight.at[0], 1)
    load_value = load(value_hbm, weight.at[1], 2)
    load_text = load(text_hbm, text, 3)

    barrier = pltpu.get_barrier_semaphore()

    def greet_group(d, carry):
        pl.semaphore_signal(barrier, inc=1, device_id={"grp": lax.rem(g + d, groups)}, device_id_type=MESH)
        return carry

    def greet_sp(d, carry):
        pl.semaphore_signal(barrier, inc=1, device_id={"sp": lax.rem(s + d, sps)}, device_id_type=MESH)
        return carry

    lax.fori_loop(1, groups, greet_group, 0)
    lax.fori_loop(1, sps, greet_sp, 0)

    senders, earlier, count = [], [], jnp.int32(0)
    for source in range(groups):
        found = jnp.int32(0)
        for r in range(runs):
            found = found + (dest[(source * runs + r) * cap] == g).astype(jnp.int32)
        senders.append(found)
        earlier.append(count)
        count = count + found
    n_senders = count
    order = []
    for b in range(groups):
        place_of = jnp.int32(0)
        for source in range(b, groups):
            hit = senders[source] * (earlier[source] == b).astype(jnp.int32)
            place_of = place_of + hit * lax.rem(g - source + groups, groups)
        order.append(jnp.minimum(place_of, groups - 1))
    heads = [dest[(g * runs + r) * cap] for r in range(runs)]

    load_vis.wait()

    def project(n, total):
        proj_copy(n).wait()
        columns = pl.ds(pl.multiple_of(n * tile, tile), tile)
        block = jnp.dot(vis[...], proj[:, columns], preferred_element_type=F32).astype(BF16).astype(F32)
        tok[:, columns] = (block * gain[:, columns]).astype(BF16)
        return total + jnp.sum(block * block, axis=1, keepdims=True)

    squares = lax.fori_loop(0, features // tile, project, jnp.zeros((vis.shape[0], 1), F32))
    tok_sq[...] = as_row(squares)
    pl.semaphore_wait(barrier, groups - 1 + sps - 1)

    def token_square_copy(j):
        return pltpu.make_async_remote_copy(
            src_ref=tok_sq, dst_ref=tok_sq_recv.at[j],
            send_sem=tsq_send_sem.at[j], recv_sem=tsq_recv_sem.at[j],
            device_id={"sp": lax.rem(s + j, sps)}, device_id_type=MESH,
        )

    lax.fori_loop(1, sps, lambda j, c: (token_square_copy(j).start(), c)[1], 0)

    def twin_copy(yc):
        return pltpu.make_async_remote_copy(
            src_ref=tok_send.at[yc], dst_ref=tok_recv.at[yc],
            send_sem=tok_send_sem.at[yc], recv_sem=tok_recv_sem.at[yc],
            device_id={"sp": twin}, device_id_type=MESH,
        )

    def token_y_copy(j, p):
        return pltpu.make_async_remote_copy(
            src_ref=tok_y_send.at[j, p], dst_ref=tok_y_recv.at[j, p],
            send_sem=tok_y_send_sem.at[j, p], recv_sem=tok_y_recv_sem.at[j, p],
            device_id={"sp": lax.rem(y + j, ys) * 2 + core}, device_id_type=MESH,
        )

    load_key.wait()
    load_value.wait()
    product = jnp.dot(tok[...], weight[other], preferred_element_type=F32).astype(BF16)
    for yc in range(ys):
        for p in range(pieces):
            at = yc * share + p * width
            tok_send[yc, p] = product[:, at:at + width]
    lax.fori_loop(1, ys + 1, lambda j, c: (twin_copy(lax.rem(y + j, ys)).start(), c)[1], 0)
    product = jnp.dot(tok[...], weight[core], preferred_element_type=F32)
    for yc in range(ys):
        for p in range(pieces):
            at = yc * share + p * width
            tok_own[yc, p] = product[:, at:at + width]

    def pass_tokens(j, carry):
        yc = lax.rem(y + j, ys)
        twin_copy(yc).wait()
        for p in range(pieces):
            tok_y_send[j, p] = (tok_own[yc, p] + tok_recv[yc, p].astype(F32)).astype(BF16)
            token_y_copy(j, p).start()
        return carry

    lax.fori_loop(1, ys, pass_tokens, 0)

    load_text.wait()
    rank_index = lax.broadcasted_iota(jnp.int32, (1, ranks), 1)
    position_of = jnp.where(rank_index < n_senders * pad, lay[:, :ranks], -1)

    def place(q):
        at = pl.ds(pl.multiple_of(q * rows, rows), rows)
        position = lax.broadcasted_iota(jnp.int32, (rows, ranks), 0) + q * rows
        hit = (position == position_of).astype(F32)
        onehot[at, :] = hit.astype(BF16)
        keep = 1.0 - jnp.max(hit, axis=1, keepdims=True)
        values = text[at, :].astype(F32)
        row_sq[q] = as_row(jnp.sum(values * values, axis=1, keepdims=True))
        text[at, :] = (values * gain[...] * keep).astype(BF16)

    def square_copy(j):
        partner = lax.rem(s + j, sps)
        return pltpu.make_async_remote_copy(
            src_ref=row_sq.at[partner], dst_ref=row_sq_recv.at[j],
            send_sem=sq_send_sem.at[j], recv_sem=sq_recv_sem.at[j],
            device_id={"sp": partner}, device_id_type=MESH,
        )

    by_share = share % 128 == 0

    def multiply(q, yc):
        at = pl.ds(pl.multiple_of(q * rows, rows), rows)
        columns = pl.ds(pl.multiple_of(yc * share, share), share)
        for kind in range(2):
            block = jnp.dot(text[at, :], weight[kind, :, columns], preferred_element_type=F32).astype(BF16)
            for p in range(pieces):
                part[yc, p, lax.rem(q, 2), q // 2, kind] = block[:, p * width:(p + 1) * width]

    def multiply_all(q):
        at = pl.ds(pl.multiple_of(q * rows, rows), rows)
        for kind in range(2):
            block = jnp.dot(text[at, :], weight[kind], preferred_element_type=F32).astype(BF16)
            for yc in range(ys):
                for p in range(pieces):
                    first = yc * share + p * width
                    part[yc, p, lax.rem(q, 2), q // 2, kind] = block[:, first:first + width]

    def core_copy(yc, p, yy):
        return pltpu.make_async_remote_copy(
            src_ref=part.at[yc, p, other, yy], dst_ref=core_recv.at[yc, p, yy],
            send_sem=core_send_sem.at[yc, p, yy], recv_sem=core_recv_sem.at[yc, p, yy],
            device_id={"sp": twin}, device_id_type=MESH,
        )

    def y_copy(yc, p, j):
        yy = lax.rem(y + j, ys)
        return pltpu.make_async_remote_copy(
            src_ref=part.at[yc, p, core, yy], dst_ref=y_recv.at[yc, p, j],
            send_sem=y_send_sem.at[yc, p, j], recv_sem=y_recv_sem.at[yc, p, j],
            device_id={"sp": yy * 2 + core}, device_id_type=MESH,
        )

    def pass_on(yc, p):
        def one(j, carry):
            yy = lax.rem(y + j, ys)
            core_copy(yc, p, yy).wait()
            pair = part[yc, p, core, yy].astype(F32) + core_recv[yc, p, yy].astype(F32)
            part[yc, p, core, yy] = pair.astype(BF16)
            y_copy(yc, p, j).start()
            return carry

        lax.fori_loop(1, ys, one, 0)

    def prepare(yy):
        def one(side, carry):
            q = yy * 2 + side
            place(q)
            if by_share:
                lax.fori_loop(1, ys, lambda j, c: (multiply(q, lax.rem(y + j, ys)), c)[1], 0)
            else:
                multiply_all(q)
            return carry

        lax.fori_loop(0, 2, one, 0)

        def send_share(j, carry):
            for p in range(pieces):
                core_copy(lax.rem(y + j, ys), p, yy).start()
            return carry

        lax.fori_loop(1, ys, send_share, 0)

    lax.fori_loop(1, ys, lambda j, c: (prepare(lax.rem(y + j, ys)), c)[1], 0)

    def gather_token_squares(j, total):
        token_square_copy(j).wait()
        return total + tok_sq_recv[j]

    total = lax.fori_loop(1, sps, gather_token_squares, tok_sq[...])
    token_scale = as_column(lax.rsqrt(total / total_features + EPS))[:, :width]

    def group_copy(p, d):
        return pltpu.make_async_remote_copy(
            src_ref=out.at[p, d], dst_ref=arrived[p].at[d],
            send_sem=out_sem.at[p, d], recv_sem=arr_sem.at[p, d],
            device_id={"grp": lax.rem(g + d, groups)}, device_id_type=MESH,
        )

    def run_for(h):
        run = jnp.int32(0)
        for r in range(1, runs):
            run = run + r * (heads[r] == h).astype(jnp.int32)
        return jnp.minimum(run, runs - 1)

    twin_copy(y).wait()
    for p in range(pieces):
        def gather_tokens(j, sums):
            token_y_copy(j, p).wait()
            return sums + tok_y_recv[j, p].astype(F32)

        sums = lax.fori_loop(1, ys, gather_tokens, tok_own[y, p] + tok_recv[y, p].astype(F32))
        tok_done[p] = (sums * token_scale).astype(BF16).reshape(runs, pad, width)
        arrived[p][0] = tok_done[p, run_for(g)]

        def send(d, carry):
            out[p, d] = tok_done[p, run_for(lax.rem(g + d, groups))]
            group_copy(p, d).start()
            return carry

        lax.fori_loop(1, groups, send, 0)
        lax.fori_loop(1, ys, lambda j, c: (pass_on(lax.rem(y + j, ys), p), c)[1], 0)

    prepare(y)
    lax.fori_loop(1, sps, lambda j, c: (square_copy(j).start(), c)[1], 0)

    if by_share:
        lax.fori_loop(0, sps, lambda q, c: (multiply(q, y), c)[1], 0)

    def place_tokens(p, side, yy):
        at = pl.ds(pl.multiple_of((yy * 2 + side) * rows, rows), rows)
        tokens = jnp.dot(onehot[at, :], ranked[...], preferred_element_type=F32)
        part[y, p, side, yy, core] = (part[y, p, side, yy, core].astype(F32) + tokens).astype(BF16)

    for p in range(pieces):
        lax.fori_loop(1, groups, lambda d, c: (group_copy(p, d).wait(), c)[1], 0)
        for b in range(groups):
            ranked[b * pad:(b + 1) * pad, :] = arrived[p][order[b]]

        def place_and_send(j, carry):
            yy = lax.rem(y + j, ys)
            place_tokens(p, other, yy)
            core_copy(y, p, yy).start()
            return carry

        lax.fori_loop(1, ys + 1, place_and_send, 0)
        lax.fori_loop(1, ys + 1, lambda j, c: (place_tokens(p, core, lax.rem(y + j, ys)), c)[1], 0)
        pass_on(y, p)

    def gather_squares(j, total):
        square_copy(j).wait()
        return total + row_sq_recv[j]

    total = lax.fori_loop(1, sps, gather_squares, row_sq[s])
    mine = pl.ds(pl.multiple_of(s * rows, rows), rows)
    visual = jnp.max(onehot[mine, :].astype(F32), axis=1, keepdims=True)
    scale = as_column(lax.rsqrt(total / total_features + EPS))[:, :width]
    scale = jnp.where(visual > 0.5, 1.0, scale)
    for p in range(pieces):
        for yc in range(ys):
            def add(j, sums):
                y_copy(yc, p, j).wait()
                return sums + y_recv[yc, p, j].astype(F32)

            core_copy(yc, p, y).wait()
            sums = part[yc, p, core, y].astype(F32) + core_recv[yc, p, y].astype(F32)
            sums = lax.fori_loop(1, ys, add, sums)
            first = yc * share + p * width
            result[0, :, first:first + width] = (sums[0] * scale).astype(BF16)
            result[1, :, first:first + width] = (sums[1] * scale).astype(BF16)


def split(both, key_out, value_out, held, in_sem, out_sem):
    loads = [pltpu.make_async_copy(both.at[i], held.at[i], in_sem.at[i]) for i in range(2)]
    stores = [pltpu.make_async_copy(held.at[i], to, out_sem.at[i]) for i, to in enumerate((key_out, value_out))]
    for copy in loads:
        copy.start()
    for copy, store in zip(loads, stores):
        copy.wait()
        store.start()
    for store in stores:
        store.wait()


def local(groups, sps, vis_feats, proj_w, text_embed, dest_group, layout, norm_gain, key_w, value_w):
    seq_len, features = text_embed.shape
    shard, raw = vis_feats.shape
    runs = groups // 2
    cap = shard // runs
    pad = -(-cap // 16) * 16
    ranked_layout = layout
    if pad != cap:
        vis_feats = jnp.pad(vis_feats.reshape(runs, cap, raw), ((0, 0), (0, pad - cap), (0, 0)))
        vis_feats = vis_feats.reshape(runs * pad, raw)
        ranked_layout = layout[0, : groups * cap].reshape(groups, cap)
        ranked_layout = jnp.pad(ranked_layout, ((0, 0), (0, pad - cap)), constant_values=-1)
        ranked_layout = ranked_layout.reshape(1, groups * pad)
    tokens = runs * pad
    cols = key_w.shape[1]
    rows = seq_len // sps
    ys = sps // 2
    width = min(128, cols // ys)
    pieces = cols // (ys * width)
    ranks = groups * pad
    dims = (groups, sps, runs, cap, pad, pieces, width)
    vmem = pl.BlockSpec(memory_space=pltpu.VMEM)
    smem = pl.BlockSpec(memory_space=pltpu.SMEM)
    anywhere = pl.BlockSpec(memory_space=pl.ANY)
    dma = pltpu.SemaphoreType.DMA
    both = pl.pallas_call(
        functools.partial(kernel, dims),
        out_shape=jax.ShapeDtypeStruct((2, rows, cols), BF16),
        in_specs=[smem, vmem, vmem] + [anywhere] * 5,
        out_specs=vmem,
        scratch_shapes=[
            pltpu.VMEM((tokens, raw), BF16),
            pltpu.VMEM((raw, features), BF16),
            pltpu.VMEM((seq_len, features), BF16),
            pltpu.VMEM((2, features, cols), BF16),
            pltpu.VMEM((tokens, features), BF16),
            pltpu.VMEM((ys, pieces, tokens, width), F32),
            pltpu.VMEM((ys, pieces, tokens, width), BF16),
            pltpu.VMEM((ys, pieces, tokens, width), BF16),
            pltpu.VMEM((ys, pieces, tokens, width), BF16),
            pltpu.VMEM((ys, pieces, tokens, width), BF16),
            pltpu.VMEM((8, tokens), F32),
            pltpu.VMEM((sps, 8, tokens), F32),
            pltpu.VMEM((pieces, runs, pad, width), BF16),
            pltpu.VMEM((pieces, groups, pad, width), BF16),
            pltpu.VMEM((ranks, width), BF16),
            pltpu.VMEM((seq_len, ranks), BF16),
            pltpu.VMEM((ys, pieces, 2, ys, 2, rows, width), BF16),
            pltpu.VMEM((ys, pieces, ys, 2, rows, width), BF16),
            pltpu.VMEM((ys, pieces, ys, 2, rows, width), BF16),
            pltpu.VMEM((sps, 8, rows), F32),
            pltpu.VMEM((sps, 8, rows), F32),
            dma((4,)), dma((features // min(256, features),)),
            dma((sps,)), dma((sps,)),
            dma((ys,)), dma((ys,)), dma((ys, pieces)), dma((ys, pieces)),
            dma((pieces, groups)), dma((pieces, groups)),
            dma((sps,)), dma((sps,)),
            dma((ys, pieces, ys)), dma((ys, pieces, ys)),
            dma((ys, pieces, ys)), dma((ys, pieces, ys)),
        ] + [pltpu.VMEM((groups, pad, width), BF16)] * pieces,
        compiler_params=pltpu.CompilerParams(
            collective_id=0, has_side_effects=True, vmem_limit_bytes=60 * 1024 * 1024
        ),
        cost_estimate=pl.CostEstimate(flops=5 * 10**9, bytes_accessed=8 * 2**20, transcendentals=0),
        name="route_project",
    )(dest_group, ranked_layout, norm_gain.reshape(1, features), vis_feats, proj_w, text_embed, key_w, value_w)
    return pl.pallas_call(
        split,
        out_shape=[jax.ShapeDtypeStruct((rows, cols), BF16)] * 2,
        in_specs=[anywhere],
        out_specs=[anywhere, anywhere],
        scratch_shapes=[pltpu.VMEM((2, rows, cols), BF16), dma((2,)), dma((2,))],
        compiler_params=pltpu.CompilerParams(vmem_limit_bytes=60 * 1024 * 1024),
        name="split_result",
    )(both)


def solution(mesh):
    return jax.shard_map(
        functools.partial(local, mesh.shape["grp"], mesh.shape["sp"]),
        mesh=mesh,
        in_specs=(
            P("grp", None),
            P(None, "sp"),
            P("grp", "sp"),
            P(),
            P("grp", None),
            P("sp"),
            P("sp", None),
            P("sp", None),
        ),
        out_specs=(P(("grp", "sp"), None), P(("grp", "sp"), None)),
        check_vma=False,
    )
```

```python
import functools

import jax
import jax.numpy as jnp
from jax import lax
from jax.experimental import pallas as pl
from jax.experimental.pallas import tpu as pltpu
from jax.sharding import PartitionSpec as P

EPS = 1e-05
MESH = pl.DeviceIdType.MESH
F32 = jnp.float32
BF16 = jnp.bfloat16


def as_row(column):
    return jnp.broadcast_to(column, (column.shape[0], 128)).T[:8]


def as_column(row):
    return jnp.broadcast_to(row[:1], (128, row.shape[1])).T


def kernel(
    dims,
    dest, lay, gain, vis_hbm, proj_hbm, text_hbm, key_hbm, value_hbm,
    result,
    vis, proj, text, weight,
    tok, tok_own, tok_send, tok_recv, tok_y_send, tok_y_recv, tok_sq, tok_sq_recv, tok_done,
    out, ranked, onehot,
    part, core_recv, y_recv, row_sq, row_sq_recv,
    load_sem, proj_sem, tsq_send_sem, tsq_recv_sem, tok_send_sem, tok_recv_sem, tok_y_send_sem, tok_y_recv_sem,
    out_sem, arr_sem, sq_send_sem, sq_recv_sem,
    core_send_sem, core_recv_sem, y_send_sem, y_recv_sem, held, result_sem,
    *arrived,
):
    groups, sps, runs, cap, pad, pieces, width = dims
    ys = sps // 2
    share = pieces * width
    g = lax.axis_index("grp")
    s = lax.axis_index("sp")
    y, core = s // 2, lax.rem(s, 2)
    other = 1 - core
    twin = y * 2 + other
    rows = part.shape[5]
    ranks = groups * pad
    features = text.shape[1]
    total_features = features * sps

    def load(source, target, index):
        copy = pltpu.make_async_copy(source, target, load_sem.at[index])
        copy.start()
        return copy

    tile = min(256, features)

    def proj_copy(n):
        columns = pl.ds(pl.multiple_of(n * tile, tile), tile)
        return pltpu.make_async_copy(proj_hbm.at[:, columns], proj.at[:, columns], proj_sem.at[n])

    load_vis = load(vis_hbm, vis, 0)
    for n in range(features // tile):
        proj_copy(n).start()
    load_key = load(key_hbm, weight.at[0], 1)
    load_value = load(value_hbm, weight.at[1], 2)

    barrier = pltpu.get_barrier_semaphore()

    def greet_group(d, carry):
        pl.semaphore_signal(barrier, inc=1, device_id={"grp": lax.rem(g + d, groups)}, device_id_type=MESH)
        return carry

    def greet_sp(d, carry):
        pl.semaphore_signal(barrier, inc=1, device_id={"sp": lax.rem(s + d, sps)}, device_id_type=MESH)
        return carry

    lax.fori_loop(1, groups, greet_group, 0)
    lax.fori_loop(1, sps, greet_sp, 0)

    senders, earlier, count = [], [], jnp.int32(0)
    for source in range(groups):
        found = jnp.int32(0)
        for r in range(runs):
            found = found + (dest[(source * runs + r) * cap] == g).astype(jnp.int32)
        senders.append(found)
        earlier.append(count)
        count = count + found
    n_senders = count
    order = []
    for b in range(groups):
        place_of = jnp.int32(0)
        for source in range(b, groups):
            hit = senders[source] * (earlier[source] == b).astype(jnp.int32)
            place_of = place_of + hit * lax.rem(g - source + groups, groups)
        order.append(jnp.minimum(place_of, groups - 1))
    heads = [dest[(g * runs + r) * cap] for r in range(runs)]

    load_vis.wait()

    squares = jnp.zeros((vis.shape[0], 1), F32)
    for n in range(features // tile):
        proj_copy(n).wait()
        if n == 0:
            load_text = load(text_hbm, text, 3)
        columns = pl.ds(n * tile, tile)
        block = jnp.dot(vis[...], proj[:, columns], preferred_element_type=F32).astype(BF16).astype(F32)
        tok[:, columns] = (block * gain[:, columns]).astype(BF16)
        squares = squares + jnp.sum(block * block, axis=1, keepdims=True)
    tok_sq[...] = as_row(squares)
    pl.semaphore_wait(barrier, groups - 1 + sps - 1)

    def token_square_copy(j):
        return pltpu.make_async_remote_copy(
            src_ref=tok_sq, dst_ref=tok_sq_recv.at[j],
            send_sem=tsq_send_sem.at[j], recv_sem=tsq_recv_sem.at[j],
            device_id={"sp": lax.rem(s + j, sps)}, device_id_type=MESH,
        )

    lax.fori_loop(1, sps, lambda j, c: (token_square_copy(j).start(), c)[1], 0)

    def twin_copy(yc):
        return pltpu.make_async_remote_copy(
            src_ref=tok_send.at[yc], dst_ref=tok_recv.at[yc],
            send_sem=tok_send_sem.at[yc], recv_sem=tok_recv_sem.at[yc],
            device_id={"sp": twin}, device_id_type=MESH,
        )

    def token_y_copy(j, p):
        return pltpu.make_async_remote_copy(
            src_ref=tok_y_send.at[j, p], dst_ref=tok_y_recv.at[j, p],
            send_sem=tok_y_send_sem.at[j, p], recv_sem=tok_y_recv_sem.at[j, p],
            device_id={"sp": lax.rem(y + j, ys) * 2 + core}, device_id_type=MESH,
        )

    load_key.wait()
    load_value.wait()
    product = jnp.dot(tok[...], weight[other], preferred_element_type=F32).astype(BF16)
    for yc in range(ys):
        for p in range(pieces):
            at = yc * share + p * width
            tok_send[yc, p] = product[:, at:at + width]
    lax.fori_loop(1, ys + 1, lambda j, c: (twin_copy(lax.rem(y + j, ys)).start(), c)[1], 0)
    product = jnp.dot(tok[...], weight[core], preferred_element_type=F32)
    for yc in range(ys):
        for p in range(pieces):
            at = yc * share + p * width
            tok_own[yc, p] = product[:, at:at + width]

    def pass_tokens(j, carry):
        yc = lax.rem(y + j, ys)
        twin_copy(yc).wait()
        for p in range(pieces):
            tok_y_send[j, p] = (tok_own[yc, p] + tok_recv[yc, p].astype(F32)).astype(BF16)
            token_y_copy(j, p).start()
        return carry

    lax.fori_loop(1, ys, pass_tokens, 0)

    load_text.wait()
    rank_index = lax.broadcasted_iota(jnp.int32, (1, ranks), 1)
    position_of = jnp.where(rank_index < n_senders * pad, lay[:, :ranks], -1)

    def place(q):
        at = pl.ds(pl.multiple_of(q * rows, rows), rows)
        position = lax.broadcasted_iota(jnp.int32, (rows, ranks), 0) + q * rows
        hit = (position == position_of).astype(F32)
        onehot[at, :] = hit.astype(BF16)
        keep = 1.0 - jnp.max(hit, axis=1, keepdims=True)
        values = text[at, :].astype(F32)
        row_sq[q] = as_row(jnp.sum(values * values, axis=1, keepdims=True))
        text[at, :] = (values * gain[...] * keep).astype(BF16)

    def square_copy(j):
        partner = lax.rem(s + j, sps)
        return pltpu.make_async_remote_copy(
            src_ref=row_sq.at[partner], dst_ref=row_sq_recv.at[j],
            send_sem=sq_send_sem.at[j], recv_sem=sq_recv_sem.at[j],
            device_id={"sp": partner}, device_id_type=MESH,
        )

    by_share = share % 128 == 0

    def multiply(q, yc):
        at = pl.ds(pl.multiple_of(q * rows, rows), rows)
        columns = pl.ds(pl.multiple_of(yc * share, share), share)
        for kind in range(2):
            block = jnp.dot(text[at, :], weight[kind, :, columns], preferred_element_type=F32).astype(BF16)
            for p in range(pieces):
                part[yc, p, lax.rem(q, 2), q // 2, kind] = block[:, p * width:(p + 1) * width]

    def multiply_all(q):
        at = pl.ds(pl.multiple_of(q * rows, rows), rows)
        for kind in range(2):
            block = jnp.dot(text[at, :], weight[kind], preferred_element_type=F32).astype(BF16)
            for yc in range(ys):
                for p in range(pieces):
                    first = yc * share + p * width
                    part[yc, p, lax.rem(q, 2), q // 2, kind] = block[:, first:first + width]

    def core_copy(yc, p, yy):
        return pltpu.make_async_remote_copy(
            src_ref=part.at[yc, p, other, yy], dst_ref=core_recv.at[yc, p, yy],
            send_sem=core_send_sem.at[yc, p, yy], recv_sem=core_recv_sem.at[yc, p, yy],
            device_id={"sp": twin}, device_id_type=MESH,
        )

    def y_copy(yc, p, j):
        yy = lax.rem(y + j, ys)
        return pltpu.make_async_remote_copy(
            src_ref=part.at[yc, p, core, yy], dst_ref=y_recv.at[yc, p, j],
            send_sem=y_send_sem.at[yc, p, j], recv_sem=y_recv_sem.at[yc, p, j],
            device_id={"sp": yy * 2 + core}, device_id_type=MESH,
        )

    def pass_on(yc, p):
        def one(j, carry):
            yy = lax.rem(y + j, ys)
            core_copy(yc, p, yy).wait()
            pair = part[yc, p, core, yy].astype(F32) + core_recv[yc, p, yy].astype(F32)
            part[yc, p, core, yy] = pair.astype(BF16)
            y_copy(yc, p, j).start()
            return carry

        lax.fori_loop(1, ys, one, 0)

    def prepare(yy):
        for side in range(2):
            q = yy * 2 + side
            place(q)
            if not by_share:
                multiply_all(q)
            elif ys == 2:
                multiply(q, 1 - y)
            else:
                lax.fori_loop(1, ys, lambda j, c: (multiply(q, lax.rem(y + j, ys)), c)[1], 0)

        def send_share(j, carry):
            for p in range(pieces):
                core_copy(lax.rem(y + j, ys), p, yy).start()
            return carry

        lax.fori_loop(1, ys, send_share, 0)

    lax.fori_loop(1, ys, lambda j, c: (prepare(lax.rem(y + j, ys)), c)[1], 0)

    def gather_token_squares(j, total):
        token_square_copy(j).wait()
        return total + tok_sq_recv[j]

    total = lax.fori_loop(1, sps, gather_token_squares, tok_sq[...])
    token_scale = as_column(lax.rsqrt(total / total_features + EPS))[:, :width]

    def group_copy(p, d):
        return pltpu.make_async_remote_copy(
            src_ref=out.at[p, d], dst_ref=arrived[p].at[d],
            send_sem=out_sem.at[p, d], recv_sem=arr_sem.at[p, d],
            device_id={"grp": lax.rem(g + d, groups)}, device_id_type=MESH,
        )

    def run_for(h):
        run = jnp.int32(0)
        for r in range(1, runs):
            run = run + r * (heads[r] == h).astype(jnp.int32)
        return jnp.minimum(run, runs - 1)

    twin_copy(y).wait()
    for p in range(pieces):
        def gather_tokens(j, sums):
            token_y_copy(j, p).wait()
            return sums + tok_y_recv[j, p].astype(F32)

        sums = lax.fori_loop(1, ys, gather_tokens, tok_own[y, p] + tok_recv[y, p].astype(F32))
        tok_done[p] = (sums * token_scale).astype(BF16).reshape(runs, pad, width)
        arrived[p][0] = tok_done[p, run_for(g)]

        def send(d, carry):
            out[p, d] = tok_done[p, run_for(lax.rem(g + d, groups))]
            group_copy(p, d).start()
            return carry

        lax.fori_loop(1, groups, send, 0)
        lax.fori_loop(1, ys, lambda j, c: (pass_on(lax.rem(y + j, ys), p), c)[1], 0)

    prepare(y)
    lax.fori_loop(1, sps, lambda j, c: (square_copy(j).start(), c)[1], 0)

    if by_share:
        lax.fori_loop(0, ys, lambda yy, c: (multiply(2 * yy, y), multiply(2 * yy + 1, y), c)[2], 0)

    def gather_squares(j, total):
        square_copy(j).wait()
        return total + row_sq_recv[j]

    total = lax.fori_loop(1, sps, gather_squares, row_sq[s])
    mine = pl.ds(pl.multiple_of(s * rows, rows), rows)
    visual = jnp.max(onehot[mine, :].astype(F32), axis=1, keepdims=True)
    scale = as_column(lax.rsqrt(total / total_features + EPS))[:, :width]
    scale = jnp.where(visual > 0.5, 1.0, scale)

    def place_tokens(p, side, yy):
        at = pl.ds(pl.multiple_of((yy * 2 + side) * rows, rows), rows)
        tokens = jnp.dot(onehot[at, :], ranked[...], preferred_element_type=F32)
        part[y, p, side, yy, core] = (part[y, p, side, yy, core].astype(F32) + tokens).astype(BF16)

    for p in range(pieces):
        lax.fori_loop(1, groups, lambda d, c: (group_copy(p, d).wait(), c)[1], 0)
        for b in range(groups):
            ranked[b * pad:(b + 1) * pad, :] = arrived[p][order[b]]

        def place_and_send(j, carry):
            yy = lax.rem(y + j, ys)
            place_tokens(p, other, yy)
            core_copy(y, p, yy).start()
            return carry

        lax.fori_loop(1, ys + 1, place_and_send, 0)
        lax.fori_loop(1, ys + 1, lambda j, c: (place_tokens(p, core, lax.rem(y + j, ys)), c)[1], 0)
        pass_on(y, p)

    def finish(yc, p, index, first):
        def add(j, sums):
            y_copy(yc, p, j).wait()
            return sums + y_recv[yc, p, j].astype(F32)

        core_copy(yc, p, y).wait()
        sums = part[yc, p, core, y].astype(F32) + core_recv[yc, p, y].astype(F32)
        sums = lax.fori_loop(1, ys, add, sums)
        columns = pl.ds(first, width)
        held[0, :, columns] = (sums[0] * scale).astype(BF16)
        held[1, :, columns] = (sums[1] * scale).astype(BF16)
        if by_share:
            result_copy(columns, index).start()

    def result_copy(columns, index):
        return pltpu.make_async_copy(held.at[:, :, columns], result.at[:, :, columns], result_sem.at[index])

    for turn in range(ys):
        for p in range(pieces):
            if by_share:
                yc = lax.rem(y + turn, ys)
                finish(yc, p, turn * pieces + p, pl.multiple_of(yc * share + p * width, width))
            else:
                finish(turn, p, 0, turn * share + p * width)
    if not by_share:
        everything = pltpu.make_async_copy(held, result, result_sem.at[0])
        everything.start()
        everything.wait()
    else:
        for turn in range(ys):
            for p in range(pieces):
                first = pl.multiple_of(lax.rem(y + turn, ys) * share + p * width, width)
                result_copy(pl.ds(first, width), turn * pieces + p).wait()


def split(both, key_out, value_out, held, in_sem, out_sem):
    loads = [pltpu.make_async_copy(both.at[i], held.at[i], in_sem.at[i]) for i in range(2)]
    stores = [pltpu.make_async_copy(held.at[i], to, out_sem.at[i]) for i, to in enumerate((key_out, value_out))]
    for copy in loads:
        copy.start()
    for copy, store in zip(loads, stores):
        copy.wait()
        store.start()
    for store in stores:
        store.wait()


def local(groups, sps, vis_feats, proj_w, text_embed, dest_group, layout, norm_gain, key_w, value_w):
    seq_len, features = text_embed.shape
    shard, raw = vis_feats.shape
    runs = groups // 2
    cap = shard // runs
    pad = -(-cap // 16) * 16
    ranked_layout = layout
    if pad != cap:
        vis_feats = jnp.pad(vis_feats.reshape(runs, cap, raw), ((0, 0), (0, pad - cap), (0, 0)))
        vis_feats = vis_feats.reshape(runs * pad, raw)
        ranked_layout = layout[0, : groups * cap].reshape(groups, cap)
        ranked_layout = jnp.pad(ranked_layout, ((0, 0), (0, pad - cap)), constant_values=-1)
        ranked_layout = ranked_layout.reshape(1, groups * pad)
    tokens = runs * pad
    cols = key_w.shape[1]
    rows = seq_len // sps
    ys = sps // 2
    width = min(128, cols // ys)
    pieces = cols // (ys * width)
    ranks = groups * pad
    dims = (groups, sps, runs, cap, pad, pieces, width)
    vmem = pl.BlockSpec(memory_space=pltpu.VMEM)
    smem = pl.BlockSpec(memory_space=pltpu.SMEM)
    anywhere = pl.BlockSpec(memory_space=pl.ANY)
    dma = pltpu.SemaphoreType.DMA
    both = pl.pallas_call(
        functools.partial(kernel, dims),
        out_shape=jax.ShapeDtypeStruct((2, rows, cols), BF16),
        in_specs=[smem, vmem, vmem] + [anywhere] * 5,
        out_specs=anywhere,
        scratch_shapes=[
            pltpu.VMEM((tokens, raw), BF16),
            pltpu.VMEM((raw, features), BF16),
            pltpu.VMEM((seq_len, features), BF16),
            pltpu.VMEM((2, features, cols), BF16),
            pltpu.VMEM((tokens, features), BF16),
            pltpu.VMEM((ys, pieces, tokens, width), F32),
            pltpu.VMEM((ys, pieces, tokens, width), BF16),
            pltpu.VMEM((ys, pieces, tokens, width), BF16),
            pltpu.VMEM((ys, pieces, tokens, width), BF16),
            pltpu.VMEM((ys, pieces, tokens, width), BF16),
            pltpu.VMEM((8, tokens), F32),
            pltpu.VMEM((sps, 8, tokens), F32),
            pltpu.VMEM((pieces, runs, pad, width), BF16),
            pltpu.VMEM((pieces, groups, pad, width), BF16),
            pltpu.VMEM((ranks, width), BF16),
            pltpu.VMEM((seq_len, ranks), BF16),
            pltpu.VMEM((ys, pieces, 2, ys, 2, rows, width), BF16),
            pltpu.VMEM((ys, pieces, ys, 2, rows, width), BF16),
            pltpu.VMEM((ys, pieces, ys, 2, rows, width), BF16),
            pltpu.VMEM((sps, 8, rows), F32),
            pltpu.VMEM((sps, 8, rows), F32),
            dma((4,)), dma((features // min(256, features),)),
            dma((sps,)), dma((sps,)),
            dma((ys,)), dma((ys,)), dma((ys, pieces)), dma((ys, pieces)),
            dma((pieces, groups)), dma((pieces, groups)),
            dma((sps,)), dma((sps,)),
            dma((ys, pieces, ys)), dma((ys, pieces, ys)),
            dma((ys, pieces, ys)), dma((ys, pieces, ys)),
            pltpu.VMEM((2, rows, cols), BF16), dma((ys * pieces,)),
        ] + [pltpu.VMEM((groups, pad, width), BF16)] * pieces,
        compiler_params=pltpu.CompilerParams(
            collective_id=0, has_side_effects=True, vmem_limit_bytes=60 * 1024 * 1024
        ),
        cost_estimate=pl.CostEstimate(flops=5 * 10**9, bytes_accessed=8 * 2**20, transcendentals=0),
        name="route_project",
    )(dest_group, ranked_layout, norm_gain.reshape(1, features), vis_feats, proj_w, text_embed, key_w, value_w)
    return pl.pallas_call(
        split,
        out_shape=[jax.ShapeDtypeStruct((rows, cols), BF16)] * 2,
        in_specs=[anywhere],
        out_specs=[anywhere, anywhere],
        scratch_shapes=[pltpu.VMEM((2, rows, cols), BF16), dma((2,)), dma((2,))],
        compiler_params=pltpu.CompilerParams(vmem_limit_bytes=60 * 1024 * 1024),
        name="split_result",
    )(both)


def solution(mesh):
    return jax.shard_map(
        functools.partial(local, mesh.shape["grp"], mesh.shape["sp"]),
        mesh=mesh,
        in_specs=(
            P("grp", None),
            P(None, "sp"),
            P("grp", "sp"),
            P(),
            P("grp", None),
            P("sp"),
            P("sp", None),
            P("sp", None),
        ),
        out_specs=(P(("grp", "sp"), None), P(("grp", "sp"), None)),
        check_vma=False,
    )
```

```python
import functools

import jax
import jax.numpy as jnp
from jax import lax
from jax.experimental import pallas as pl
from jax.experimental.pallas import tpu as pltpu
from jax.sharding import PartitionSpec as P

EPS = 1e-05
MESH = pl.DeviceIdType.MESH
F32 = jnp.float32
BF16 = jnp.bfloat16


def as_row(column):
    return jnp.broadcast_to(column, (column.shape[0], 128)).T[:8]


def as_column(row):
    return jnp.broadcast_to(row[:1], (128, row.shape[1])).T


def kernel(
    dims,
    dest, lay, gain, vis_hbm, proj_hbm, text_hbm, key_hbm, value_hbm,
    result,
    vis, proj, text, weight,
    tok, tok_own, tok_send, tok_recv, tok_y_send, tok_y_recv, tok_sq, tok_sq_recv, tok_done,
    out, ranked, onehot,
    part, core_recv, y_recv, row_sq, row_sq_recv,
    load_sem, proj_sem, tsq_send_sem, tsq_recv_sem, tok_send_sem, tok_recv_sem, tok_y_send_sem, tok_y_recv_sem,
    out_sem, arr_sem, sq_send_sem, sq_recv_sem,
    core_send_sem, core_recv_sem, y_send_sem, y_recv_sem, held, result_sem,
    *arrived,
):
    groups, sps, runs, cap, pad, pieces, width = dims
    ys = sps // 2
    share = pieces * width
    g = lax.axis_index("grp")
    s = lax.axis_index("sp")
    y, core = s // 2, lax.rem(s, 2)
    other = 1 - core
    twin = y * 2 + other
    rows = part.shape[5]
    ranks = groups * pad
    features = text.shape[1]
    total_features = features * sps

    def load(source, target, index):
        copy = pltpu.make_async_copy(source, target, load_sem.at[index])
        copy.start()
        return copy

    tile = min(256, features)

    def proj_copy(n):
        columns = pl.ds(pl.multiple_of(n * tile, tile), tile)
        return pltpu.make_async_copy(proj_hbm.at[:, columns], proj.at[:, columns], proj_sem.at[n])

    load_vis = load(vis_hbm, vis, 0)
    for n in range(features // tile):
        proj_copy(n).start()
    load_key = load(key_hbm, weight.at[0], 1)
    load_value = load(value_hbm, weight.at[1], 2)
    load_text = load(text_hbm, text, 3)

    barrier = pltpu.get_barrier_semaphore()

    def greet_group(d, carry):
        pl.semaphore_signal(barrier, inc=1, device_id={"grp": lax.rem(g + d, groups)}, device_id_type=MESH)
        return carry

    def greet_sp(d, carry):
        pl.semaphore_signal(barrier, inc=1, device_id={"sp": lax.rem(s + d, sps)}, device_id_type=MESH)
        return carry

    lax.fori_loop(1, groups, greet_group, 0)
    lax.fori_loop(1, sps, greet_sp, 0)

    senders, earlier, count = [], [], jnp.int32(0)
    for source in range(groups):
        found = jnp.int32(0)
        for r in range(runs):
            found = found + (dest[(source * runs + r) * cap] == g).astype(jnp.int32)
        senders.append(found)
        earlier.append(count)
        count = count + found
    n_senders = count
    order = []
    for b in range(groups):
        place_of = jnp.int32(0)
        for source in range(b, groups):
            hit = senders[source] * (earlier[source] == b).astype(jnp.int32)
            place_of = place_of + hit * lax.rem(g - source + groups, groups)
        order.append(jnp.minimum(place_of, groups - 1))
    heads = [dest[(g * runs + r) * cap] for r in range(runs)]

    load_vis.wait()

    def project(n, total):
        proj_copy(n).wait()
        columns = pl.ds(pl.multiple_of(n * tile, tile), tile)
        block = jnp.dot(vis[...], proj[:, columns], preferred_element_type=F32).astype(BF16).astype(F32)
        tok[:, columns] = (block * gain[:, columns]).astype(BF16)
        return total + jnp.sum(block * block, axis=1, keepdims=True)

    squares = lax.fori_loop(0, features // tile, project, jnp.zeros((vis.shape[0], 1), F32))
    tok_sq[...] = as_row(squares)
    pl.semaphore_wait(barrier, groups - 1 + sps - 1)

    def token_square_copy(j):
        return pltpu.make_async_remote_copy(
            src_ref=tok_sq, dst_ref=tok_sq_recv.at[j],
            send_sem=tsq_send_sem.at[j], recv_sem=tsq_recv_sem.at[j],
            device_id={"sp": lax.rem(s + j, sps)}, device_id_type=MESH,
        )

    lax.fori_loop(1, sps, lambda j, c: (token_square_copy(j).start(), c)[1], 0)

    def twin_copy(yc):
        return pltpu.make_async_remote_copy(
            src_ref=tok_send.at[yc], dst_ref=tok_recv.at[yc],
            send_sem=tok_send_sem.at[yc], recv_sem=tok_recv_sem.at[yc],
            device_id={"sp": twin}, device_id_type=MESH,
        )

    def token_y_copy(j, p):
        return pltpu.make_async_remote_copy(
            src_ref=tok_y_send.at[j, p], dst_ref=tok_y_recv.at[j, p],
            send_sem=tok_y_send_sem.at[j, p], recv_sem=tok_y_recv_sem.at[j, p],
            device_id={"sp": lax.rem(y + j, ys) * 2 + core}, device_id_type=MESH,
        )

    load_key.wait()
    load_value.wait()
    product = jnp.dot(tok[...], weight[other], preferred_element_type=F32).astype(BF16)
    for yc in range(ys):
        for p in range(pieces):
            at = yc * share + p * width
            tok_send[yc, p] = product[:, at:at + width]
    lax.fori_loop(1, ys + 1, lambda j, c: (twin_copy(lax.rem(y + j, ys)).start(), c)[1], 0)
    product = jnp.dot(tok[...], weight[core], preferred_element_type=F32)
    for yc in range(ys):
        for p in range(pieces):
            at = yc * share + p * width
            tok_own[yc, p] = product[:, at:at + width]

    def pass_tokens(j, carry):
        yc = lax.rem(y + j, ys)
        twin_copy(yc).wait()
        for p in range(pieces):
            tok_y_send[j, p] = (tok_own[yc, p] + tok_recv[yc, p].astype(F32)).astype(BF16)
            token_y_copy(j, p).start()
        return carry

    lax.fori_loop(1, ys, pass_tokens, 0)

    load_text.wait()
    rank_index = lax.broadcasted_iota(jnp.int32, (1, ranks), 1)
    position_of = jnp.where(rank_index < n_senders * pad, lay[:, :ranks], -1)

    def place(q):
        at = pl.ds(pl.multiple_of(q * rows, rows), rows)
        position = lax.broadcasted_iota(jnp.int32, (rows, ranks), 0) + q * rows
        hit = (position == position_of).astype(F32)
        onehot[at, :] = hit.astype(BF16)
        keep = 1.0 - jnp.max(hit, axis=1, keepdims=True)
        values = text[at, :].astype(F32)
        row_sq[q] = as_row(jnp.sum(values * values, axis=1, keepdims=True))
        text[at, :] = (values * gain[...] * keep).astype(BF16)

    def square_copy(j):
        partner = lax.rem(s + j, sps)
        return pltpu.make_async_remote_copy(
            src_ref=row_sq.at[partner], dst_ref=row_sq_recv.at[j],
            send_sem=sq_send_sem.at[j], recv_sem=sq_recv_sem.at[j],
            device_id={"sp": partner}, device_id_type=MESH,
        )

    by_share = share % 128 == 0

    def multiply(q, yc):
        at = pl.ds(pl.multiple_of(q * rows, rows), rows)
        columns = pl.ds(pl.multiple_of(yc * share, share), share)
        for kind in range(2):
            block = jnp.dot(text[at, :], weight[kind, :, columns], preferred_element_type=F32).astype(BF16)
            for p in range(pieces):
                part[yc, p, lax.rem(q, 2), q // 2, kind] = block[:, p * width:(p + 1) * width]

    def multiply_all(q):
        at = pl.ds(pl.multiple_of(q * rows, rows), rows)
        for kind in range(2):
            block = jnp.dot(text[at, :], weight[kind], preferred_element_type=F32).astype(BF16)
            for yc in range(ys):
                for p in range(pieces):
                    first = yc * share + p * width
                    part[yc, p, lax.rem(q, 2), q // 2, kind] = block[:, first:first + width]

    def core_copy(yc, p, yy):
        return pltpu.make_async_remote_copy(
            src_ref=part.at[yc, p, other, yy], dst_ref=core_recv.at[yc, p, yy],
            send_sem=core_send_sem.at[yc, p, yy], recv_sem=core_recv_sem.at[yc, p, yy],
            device_id={"sp": twin}, device_id_type=MESH,
        )

    def y_copy(yc, p, j):
        yy = lax.rem(y + j, ys)
        return pltpu.make_async_remote_copy(
            src_ref=part.at[yc, p, core, yy], dst_ref=y_recv.at[yc, p, j],
            send_sem=y_send_sem.at[yc, p, j], recv_sem=y_recv_sem.at[yc, p, j],
            device_id={"sp": yy * 2 + core}, device_id_type=MESH,
        )

    def pass_on(yc, p):
        def one(j, carry):
            yy = lax.rem(y + j, ys)
            core_copy(yc, p, yy).wait()
            pair = part[yc, p, core, yy].astype(F32) + core_recv[yc, p, yy].astype(F32)
            part[yc, p, core, yy] = pair.astype(BF16)
            y_copy(yc, p, j).start()
            return carry

        lax.fori_loop(1, ys, one, 0)

    def prepare(yy):
        def one(side, carry):
            q = yy * 2 + side
            place(q)
            if by_share:
                lax.fori_loop(1, ys, lambda j, c: (multiply(q, lax.rem(y + j, ys)), c)[1], 0)
            else:
                multiply_all(q)
            return carry

        lax.fori_loop(0, 2, one, 0)

        def send_share(j, carry):
            for p in range(pieces):
                core_copy(lax.rem(y + j, ys), p, yy).start()
            return carry

        lax.fori_loop(1, ys, send_share, 0)

    lax.fori_loop(1, ys, lambda j, c: (prepare(lax.rem(y + j, ys)), c)[1], 0)

    def gather_token_squares(j, total):
        token_square_copy(j).wait()
        return total + tok_sq_recv[j]

    total = lax.fori_loop(1, sps, gather_token_squares, tok_sq[...])
    token_scale = as_column(lax.rsqrt(total / total_features + EPS))[:, :width]

    def group_copy(p, d):
        return pltpu.make_async_remote_copy(
            src_ref=out.at[p, d], dst_ref=arrived[p].at[d],
            send_sem=out_sem.at[p, d], recv_sem=arr_sem.at[p, d],
            device_id={"grp": lax.rem(g + d, groups)}, device_id_type=MESH,
        )

    def run_for(h):
        run = jnp.int32(0)
        for r in range(1, runs):
            run = run + r * (heads[r] == h).astype(jnp.int32)
        return jnp.minimum(run, runs - 1)

    twin_copy(y).wait()
    for p in range(pieces):
        def gather_tokens(j, sums):
            token_y_copy(j, p).wait()
            return sums + tok_y_recv[j, p].astype(F32)

        sums = lax.fori_loop(1, ys, gather_tokens, tok_own[y, p] + tok_recv[y, p].astype(F32))
        tok_done[p] = (sums * token_scale).astype(BF16).reshape(runs, pad, width)
        arrived[p][0] = tok_done[p, run_for(g)]

        def send(d, carry):
            out[p, d] = tok_done[p, run_for(lax.rem(g + d, groups))]
            group_copy(p, d).start()
            return carry

        lax.fori_loop(1, groups, send, 0)
        lax.fori_loop(1, ys, lambda j, c: (pass_on(lax.rem(y + j, ys), p), c)[1], 0)

    prepare(y)
    lax.fori_loop(1, sps, lambda j, c: (square_copy(j).start(), c)[1], 0)

    if by_share:
        lax.fori_loop(0, sps, lambda q, c: (multiply(q, y), c)[1], 0)

    def gather_squares(j, total):
        square_copy(j).wait()
        return total + row_sq_recv[j]

    total = lax.fori_loop(1, sps, gather_squares, row_sq[s])
    mine = pl.ds(pl.multiple_of(s * rows, rows), rows)
    visual = jnp.max(onehot[mine, :].astype(F32), axis=1, keepdims=True)
    scale = as_column(lax.rsqrt(total / total_features + EPS))[:, :width]
    scale = jnp.where(visual > 0.5, 1.0, scale)

    def place_tokens(p, side, yy):
        at = pl.ds(pl.multiple_of((yy * 2 + side) * rows, rows), rows)
        tokens = jnp.dot(onehot[at, :], ranked[...], preferred_element_type=F32)
        part[y, p, side, yy, core] = (part[y, p, side, yy, core].astype(F32) + tokens).astype(BF16)

    for p in range(pieces):
        lax.fori_loop(1, groups, lambda d, c: (group_copy(p, d).wait(), c)[1], 0)
        for b in range(groups):
            ranked[b * pad:(b + 1) * pad, :] = arrived[p][order[b]]

        def place_and_send(j, carry):
            yy = lax.rem(y + j, ys)
            place_tokens(p, other, yy)
            core_copy(y, p, yy).start()
            return carry

        lax.fori_loop(1, ys + 1, place_and_send, 0)
        lax.fori_loop(1, ys + 1, lambda j, c: (place_tokens(p, core, lax.rem(y + j, ys)), c)[1], 0)
        pass_on(y, p)

    def finish(yc, p, index, first):
        def add(j, sums):
            y_copy(yc, p, j).wait()
            return sums + y_recv[yc, p, j].astype(F32)

        core_copy(yc, p, y).wait()
        sums = part[yc, p, core, y].astype(F32) + core_recv[yc, p, y].astype(F32)
        sums = lax.fori_loop(1, ys, add, sums)
        columns = pl.ds(first, width)
        held[0, :, columns] = (sums[0] * scale).astype(BF16)
        held[1, :, columns] = (sums[1] * scale).astype(BF16)
        if by_share:
            result_copy(columns, index).start()

    def result_copy(columns, index):
        return pltpu.make_async_copy(held.at[:, :, columns], result.at[:, :, columns], result_sem.at[index])

    for turn in range(ys):
        for p in range(pieces):
            if by_share:
                yc = lax.rem(y + turn, ys)
                finish(yc, p, turn * pieces + p, pl.multiple_of(yc * share + p * width, width))
            else:
                finish(turn, p, 0, turn * share + p * width)
    if not by_share:
        everything = pltpu.make_async_copy(held, result, result_sem.at[0])
        everything.start()
        everything.wait()
    else:
        for turn in range(ys):
            for p in range(pieces):
                first = pl.multiple_of(lax.rem(y + turn, ys) * share + p * width, width)
                result_copy(pl.ds(first, width), turn * pieces + p).wait()


def split(both, key_out, value_out, held, in_sem, out_sem):
    loads = [pltpu.make_async_copy(both.at[i], held.at[i], in_sem.at[i]) for i in range(2)]
    stores = [pltpu.make_async_copy(held.at[i], to, out_sem.at[i]) for i, to in enumerate((key_out, value_out))]
    for copy in loads:
        copy.start()
    for copy, store in zip(loads, stores):
        copy.wait()
        store.start()
    for store in stores:
        store.wait()


def local(groups, sps, vis_feats, proj_w, text_embed, dest_group, layout, norm_gain, key_w, value_w):
    seq_len, features = text_embed.shape
    shard, raw = vis_feats.shape
    runs = groups // 2
    cap = shard // runs
    pad = -(-cap // 16) * 16
    ranked_layout = layout
    if pad != cap:
        vis_feats = jnp.pad(vis_feats.reshape(runs, cap, raw), ((0, 0), (0, pad - cap), (0, 0)))
        vis_feats = vis_feats.reshape(runs * pad, raw)
        ranked_layout = layout[0, : groups * cap].reshape(groups, cap)
        ranked_layout = jnp.pad(ranked_layout, ((0, 0), (0, pad - cap)), constant_values=-1)
        ranked_layout = ranked_layout.reshape(1, groups * pad)
    tokens = runs * pad
    cols = key_w.shape[1]
    rows = seq_len // sps
    ys = sps // 2
    width = min(128, cols // ys)
    pieces = cols // (ys * width)
    ranks = groups * pad
    dims = (groups, sps, runs, cap, pad, pieces, width)
    vmem = pl.BlockSpec(memory_space=pltpu.VMEM)
    smem = pl.BlockSpec(memory_space=pltpu.SMEM)
    anywhere = pl.BlockSpec(memory_space=pl.ANY)
    dma = pltpu.SemaphoreType.DMA
    both = pl.pallas_call(
        functools.partial(kernel, dims),
        out_shape=jax.ShapeDtypeStruct((2, rows, cols), BF16),
        in_specs=[smem, vmem, vmem] + [anywhere] * 5,
        out_specs=anywhere,
        scratch_shapes=[
            pltpu.VMEM((tokens, raw), BF16),
            pltpu.VMEM((raw, features), BF16),
            pltpu.VMEM((seq_len, features), BF16),
            pltpu.VMEM((2, features, cols), BF16),
            pltpu.VMEM((tokens, features), BF16),
            pltpu.VMEM((ys, pieces, tokens, width), F32),
            pltpu.VMEM((ys, pieces, tokens, width), BF16),
            pltpu.VMEM((ys, pieces, tokens, width), BF16),
            pltpu.VMEM((ys, pieces, tokens, width), BF16),
            pltpu.VMEM((ys, pieces, tokens, width), BF16),
            pltpu.VMEM((8, tokens), F32),
            pltpu.VMEM((sps, 8, tokens), F32),
            pltpu.VMEM((pieces, runs, pad, width), BF16),
            pltpu.VMEM((pieces, groups, pad, width), BF16),
            pltpu.VMEM((ranks, width), BF16),
            pltpu.VMEM((seq_len, ranks), BF16),
            pltpu.VMEM((ys, pieces, 2, ys, 2, rows, width), BF16),
            pltpu.VMEM((ys, pieces, ys, 2, rows, width), BF16),
            pltpu.VMEM((ys, pieces, ys, 2, rows, width), BF16),
            pltpu.VMEM((sps, 8, rows), F32),
            pltpu.VMEM((sps, 8, rows), F32),
            dma((4,)), dma((features // min(256, features),)),
            dma((sps,)), dma((sps,)),
            dma((ys,)), dma((ys,)), dma((ys, pieces)), dma((ys, pieces)),
            dma((pieces, groups)), dma((pieces, groups)),
            dma((sps,)), dma((sps,)),
            dma((ys, pieces, ys)), dma((ys, pieces, ys)),
            dma((ys, pieces, ys)), dma((ys, pieces, ys)),
            pltpu.VMEM((2, rows, cols), BF16), dma((ys * pieces,)),
        ] + [pltpu.VMEM((groups, pad, width), BF16)] * pieces,
        compiler_params=pltpu.CompilerParams(
            collective_id=0, has_side_effects=True, vmem_limit_bytes=60 * 1024 * 1024
        ),
        cost_estimate=pl.CostEstimate(flops=5 * 10**9, bytes_accessed=8 * 2**20, transcendentals=0),
        name="route_project",
    )(dest_group, ranked_layout, norm_gain.reshape(1, features), vis_feats, proj_w, text_embed, key_w, value_w)
    return pl.pallas_call(
        split,
        out_shape=[jax.ShapeDtypeStruct((rows, cols), BF16)] * 2,
        in_specs=[anywhere],
        out_specs=[anywhere, anywhere],
        scratch_shapes=[pltpu.VMEM((2, rows, cols), BF16), dma((2,)), dma((2,))],
        compiler_params=pltpu.CompilerParams(vmem_limit_bytes=60 * 1024 * 1024),
        name="split_result",
    )(both)


def solution(mesh):
    return jax.shard_map(
        functools.partial(local, mesh.shape["grp"], mesh.shape["sp"]),
        mesh=mesh,
        in_specs=(
            P("grp", None),
            P(None, "sp"),
            P("grp", "sp"),
            P(),
            P("grp", None),
            P("sp"),
            P("sp", None),
            P("sp", None),
        ),
        out_specs=(P(("grp", "sp"), None), P(("grp", "sp"), None)),
        check_vma=False,
    )
```
